32 devices in a mesh: groups: 2 (over x), ep: 4 (over y, core), tp: 4 (over z).
Axes of the slice: x: 2, y: 2, z: 4, core: 2. Of those that a mesh axis runs over, the one named last changes fastest.
Arguments:
- tokens: bfloat16 [1024, 3584], P(('groups', 'ep')), parts along dimension 0, may hold values from -6 to 6
- expert_ids: int32 [1024, 8], P(('groups', 'ep')), parts along dimension 0, may hold values from 0 to 9, as said below
- route_weights: float32 [1024, 8], P(('groups', 'ep')), parts along dimension 0, may hold values from 0.05 to 1
- hot_list: int32 [4], P('groups'), parts along dimension 0, may hold values from 0 to 9, as said below
- cold_gate: bfloat16 [8, 3584, 1024], P('ep', None, 'tp'), may hold values from -0.09375 to 0.09375
- cold_up: bfloat16 [8, 3584, 1024], P('ep', None, 'tp'), may hold values from -0.09375 to 0.09375
- cold_down: bfloat16 [8, 1024, 3584], P('ep', 'tp'), may hold values from -0.1875 to 0.1875
- hot_gate: bfloat16 [2, 3584, 1024], P(None, None, 'tp'), may hold values from -0.09375 to 0.09375
- hot_up: bfloat16 [2, 3584, 1024], P(None, None, 'tp'), may hold values from -0.09375 to 0.09375
- hot_down: bfloat16 [2, 1024, 3584], P(None, 'tp'), may hold values from -0.1875 to 0.1875
Outputs:
- mixed: bfloat16 [1024, 3584], P(('groups', 'ep'), 'tp'), parts along dimension 0
The draws below stay inside these ranges and needn't reach their ends.
There are 2 independent parts, one for each index of `groups`. The reference program is written for one: setup_inputs(seed, part) draws one part's arguments, and reference() takes and returns one part's arrays. A program takes and returns all parts, laid end to end along the dimension named above; an argument that names none is the same for every part. Nothing has to cross between parts.
Inputs may be any that keep to these rules, and one draw needn't show every extreme that they name: `expert_ids`: each row names 8 different experts. In each block of 128 rows (the tokens of one index of ep) no cold expert is named by more than 128 rows, and one cold expert, the same in every block, is named by exactly 128 rows. `hot_list`: 2 different expert ids in rising order; the last is always 10 - 1.
All inputs are finite; a program needn't handle non-finite values.
Results may differ from the reference program's by a relative error of at most 0.012.
Values may be sent and summed in bfloat16 or wider, within the bound.
A program may use at most 128 MiB of HBM per device.

```python
import math
import jax
import jax.numpy as jnp
from jax import lax

D = 3584
FF = 1024
TOP = 8
HOT = 2
TOK_EP = 128
COLD = 8
EXPERTS = 10
TOKENS = 512
FF_DEV = 256
COLD_ROWS = 832
CAP = 128
N_TP = 4


def routing_draw(key):
    other_order = jax.random.permutation(jax.random.fold_in(key, 11), EXPERTS - 1)
    last_id = jnp.full((1,), EXPERTS - 1, jnp.int32)
    hot_ids = jnp.sort(jnp.concatenate([other_order[:HOT - 1].astype(jnp.int32), last_id])).astype(jnp.int32)
    experts_all = jnp.arange(EXPERTS, dtype=jnp.int32)
    matches = experts_all[:, None] == hot_ids[None, :]
    is_hot = jnp.any(matches, axis=1)
    hot_place = jnp.sum(jnp.where(matches, jnp.arange(HOT, dtype=jnp.int32)[None, :], 0), axis=1)
    hot_below = jnp.sum((hot_ids[None, :] < experts_all[:, None]).astype(jnp.int32), axis=1)
    cold_place = jnp.clip(experts_all - hot_below, 0, COLD - 1)
    full_cold = jax.random.randint(jax.random.fold_in(key, 12), (), 0, COLD)
    spare_rows = COLD_ROWS - CAP
    base_load = spare_rows // (COLD - 1)
    extra_rows = spare_rows - base_load * (COLD - 1)
    swing_most = min(base_load // 2, CAP - base_load - 1)
    pair_count = (COLD - 1) // 2

    def one_block(block_index):
        block_key = jax.random.fold_in(jax.random.fold_in(key, 13), block_index)
        hot_shift = jax.random.randint(jax.random.fold_in(block_key, 1), (), 0, TOK_EP // 4)
        shift_sign = 1 - 2 * (jnp.arange(HOT, dtype=jnp.int32) % 2)
        hot_loads = 3 * TOK_EP // 4 + hot_shift * shift_sign
        rest_loads = base_load + (jnp.arange(COLD - 1) < extra_rows).astype(jnp.int32)
        load_moves = jax.random.randint(jax.random.fold_in(block_key, 2), (pair_count,), 0, swing_most + 1)
        load_delta = jnp.zeros((COLD - 1,), jnp.int32)
        load_delta = load_delta.at[0:2 * pair_count:2].add(load_moves).at[1:2 * pair_count:2].add(-load_moves)
        rest_loads = (rest_loads + load_delta)[jax.random.permutation(jax.random.fold_in(block_key, 3), COLD - 1)]
        others = jnp.arange(COLD - 1, dtype=jnp.int32)
        others = others + (others >= full_cold).astype(jnp.int32)
        cold_loads = jnp.zeros((COLD,), jnp.int32).at[others].set(rest_loads).at[full_cold].set(CAP)
        expert_loads = jnp.where(is_hot, hot_loads[hot_place], cold_loads[cold_place])
        load_ends = jnp.cumsum(expert_loads)
        positions = jnp.arange(TOK_EP * TOP, dtype=jnp.int32)
        chosen = jnp.sum((positions[:, None] >= load_ends[None, :]).astype(jnp.int32), axis=1)
        pick_table = chosen.reshape(TOP, TOK_EP).T
        pick_table = pick_table[jax.random.permutation(jax.random.fold_in(block_key, 4), TOK_EP)]
        scores = jax.random.randint(jax.random.fold_in(block_key, 5), (TOK_EP, TOP), 0, 1 << 20) * TOP + jnp.arange(TOP)
        slot_order = jnp.argsort(scores, axis=1)
        return jnp.take_along_axis(pick_table, slot_order, axis=1)
    blocks = TOKENS // TOK_EP
    pick_ids = jax.vmap(one_block)(jnp.arange(blocks)).reshape(TOKENS, TOP)
    return (hot_ids, pick_ids.astype(jnp.int32))


def draw_hot_list(key, part):
    hot_ids, pick_ids = routing_draw(key)
    return hot_ids


def draw_expert_ids(key, part):
    hot_ids, pick_ids = routing_draw(key)
    return pick_ids


def shard_levels(stream_key, shape, shards, smallest, largest):
    loudness, own = 1.0, jax.random.fold_in(stream_key, 6)
    for axis_at, blocks in shards:
        draws = jnp.exp(jax.random.uniform(jax.random.fold_in(own, axis_at), (blocks,), jnp.float32, smallest / len(shards), largest / len(shards)))
        loudness = loudness * jnp.repeat(draws, shape[axis_at] // blocks).reshape([-1 if axis == axis_at else 1 for axis in range(len(shape))])
    return loudness


def centred(own_key, dims, scale, limit, split=(), held_as=jnp.bfloat16):
    loudness = shard_levels(own_key, dims, split, -0.22, 0.18) if split else 1.0
    array = jax.random.normal(own_key, dims, jnp.float32) * scale * loudness
    return jnp.minimum(jnp.maximum(array, -limit), limit).astype(held_as)


def setup_inputs(seed: int = 0, part: int = 0) -> dict:
    key_list = jax.random.split(jax.random.key(seed), 11)
    part_keys = jax.random.split(jax.random.fold_in(key_list[10], part), 11)
    tokens = centred(part_keys[0], (TOKENS, D), 1.0, 6.0, ((0, 4),))
    expert_ids = draw_expert_ids(jax.random.fold_in(jax.random.fold_in(key_list[10], part), 71), part)
    route_weights = jnp.clip(jnp.exp(math.log(1.0) - 2.9957323 * jax.random.uniform(part_keys[2], (TOKENS, TOP), jnp.float32) ** shard_levels(part_keys[2], (TOKENS, TOP), ((0, 4),), -0.2, 0.2)), 0.05, 1.0)
    hot_list = draw_hot_list(jax.random.fold_in(jax.random.fold_in(key_list[10], part), 71), part)
    cold_gate = centred(key_list[4], (COLD, D, FF), D ** -0.5, 0.09375, ((0, 4), (2, 4)))
    cold_up = centred(key_list[5], (COLD, D, FF), D ** -0.5, 0.09375, ((0, 4), (2, 4)))
    cold_down = centred(key_list[6], (COLD, FF, D), FF ** -0.5, 0.1875, ((0, 4), (1, 4)))
    hot_gate = centred(key_list[7], (HOT, D, FF), D ** -0.5, 0.09375, ((2, 4),))
    hot_up = centred(key_list[8], (HOT, D, FF), D ** -0.5, 0.09375, ((2, 4),))
    hot_down = centred(key_list[9], (HOT, FF, D), FF ** -0.5, 0.1875, ((1, 4),))
    return {"tokens": tokens, "expert_ids": expert_ids, "route_weights": route_weights, "hot_list": hot_list, "cold_gate": cold_gate, "cold_up": cold_up, "cold_down": cold_down, "hot_gate": hot_gate, "hot_up": hot_up, "hot_down": hot_down}


ROUTE_SCALE = 2.5


def route_tables(pick_ids, weights, hot_list, cold_count, capacity):
    scaled = ROUTE_SCALE * weights / jnp.sum(weights, axis=1, keepdims=True)
    is_hot = pick_ids[:, :, None] == hot_list[None, None, :]
    hot_coef = jnp.sum(jnp.where(is_hot, scaled[:, :, None], jnp.float32(0.0)), axis=1)
    hot_below = jnp.sum((hot_list[None, None, :] < pick_ids[:, :, None]).astype(jnp.int32), axis=2)
    any_hot = jnp.any(is_hot, axis=2)
    cold_slot = jnp.where(any_hot, -1, pick_ids - hot_below).astype(jnp.int32)
    onehot = cold_slot[:, :, None] == jnp.arange(cold_count, dtype=jnp.int32)[None, None, :]
    per_token = jnp.sum(onehot.astype(jnp.int32), axis=1)
    before = jnp.cumsum(per_token, axis=0) - per_token
    pick_rank = jnp.sum(jnp.where(onehot, before[:, None, :], 0), axis=2).astype(jnp.int32)
    position = jnp.where(any_hot, -1, cold_slot * capacity + pick_rank).astype(jnp.int32)
    placed = position[:, :, None] == jnp.arange(cold_count * capacity, dtype=jnp.int32)[None, None, :]
    dispatch = jnp.any(placed, axis=1)
    combine = jnp.sum(jnp.where(placed, scaled[:, :, None], jnp.float32(0.0)), axis=1)
    return hot_coef, dispatch, combine


def cold_expert(operands):
    expert_rows, gate_w, up_w, down_w = operands
    gate_acts = jnp.dot(expert_rows, gate_w, preferred_element_type=jnp.float32)
    up_acts = jnp.dot(expert_rows, up_w, preferred_element_type=jnp.float32)
    hidden = (jax.nn.silu(gate_acts) * up_acts).astype(jnp.bfloat16)
    pieces = jnp.einsum("rbf,bfd->brd", hidden.reshape(-1, N_TP, FF_DEV).astype(jnp.float32),
                        down_w.reshape(N_TP, FF_DEV, D).astype(jnp.float32),
                        precision=lax.Precision.HIGHEST)
    rounded = lax.optimization_barrier(pieces.astype(jnp.bfloat16))
    return jnp.sum(rounded.astype(jnp.float32), axis=0)


def reference(tokens, expert_ids, route_weights, hot_list, cold_gate, cold_up, cold_down, hot_gate, hot_up, hot_down):
    blocks = TOKENS // TOK_EP

    def tables(pick_ids, weights):
        return route_tables(pick_ids, weights, hot_list, COLD, CAP)

    hot_coef, dispatch, combine = jax.vmap(tables)(expert_ids.reshape(blocks, TOK_EP, TOP),
                                                   route_weights.reshape(blocks, TOK_EP, TOP))
    token_blocks = tokens.reshape(blocks, TOK_EP, D)
    buffers = jnp.einsum("btr,btd->brd", dispatch.astype(jnp.float32), token_blocks.astype(jnp.float32),
                         precision=lax.Precision.HIGHEST).astype(jnp.bfloat16)
    expert_rows = buffers.reshape(blocks, COLD, CAP, D).transpose(1, 0, 2, 3).reshape(COLD, blocks * CAP, D)
    outputs = lax.map(cold_expert, (expert_rows, cold_gate, cold_up, cold_down))
    outputs = outputs.reshape(COLD, blocks, CAP, D).transpose(1, 0, 2, 3).reshape(blocks, COLD * CAP, D)
    cold_part = jnp.einsum("btr,brd->btd", combine, outputs, precision=lax.Precision.HIGHEST).reshape(TOKENS, D)
    flat_coef = hot_coef.reshape(TOKENS, HOT)
    hot_total = jnp.zeros((TOKENS, D), jnp.float32)
    for which in range(HOT):
        gate_acts = jnp.dot(tokens, hot_gate[which], preferred_element_type=jnp.float32)
        up_acts = jnp.dot(tokens, hot_up[which], preferred_element_type=jnp.float32)
        hidden = (jax.nn.silu(gate_acts) * up_acts).astype(jnp.bfloat16)
        result = jnp.dot(hidden, hot_down[which], preferred_element_type=jnp.float32)
        hot_total = hot_total + flat_coef[:, which:which + 1] * result
    return (hot_total + cold_part).astype(jnp.bfloat16)
```

```python
import functools

import jax
import jax.numpy as jnp
from jax import lax
from jax.experimental import pallas as pl
from jax.experimental.pallas import tpu as pltpu
from jax.sharding import PartitionSpec as P

ROUTE_SCALE = 2.5
MESH = pl.DeviceIdType.MESH
SPLITS = 4


def each(count, step):
    if count <= 4:
        for index in range(count):
            step(index)
    else:
        pl.loop(0, count)(step)


def layer_kernel(
    n_ep, n_tp,
    tok_hbm, ids_ref, weights_ref, hot_ref, cg, cu, cd, hg, hu, hd,
    out_ref,
    tok_all, wg, wu, vg, vu, wd, hid, hot_hid, coef_out, coef_in, part, own_part,
    core_out, core_in, y_out, y_in, z_out, z_in,
    w_sem, tok_sem, coef_sem, blk_sem, yt_sem, zt_sem, ct_sem, core_sem, y_sem, z_sem,
):
    rows, width = tok_hbm.shape
    cold, _, ff = wg.shape
    hot = vg.shape[0]
    piece = out_ref.shape[1]
    ny = n_ep // 2
    half = rows // 2
    run = half // SPLITS
    ep, tp = lax.axis_index("ep"), lax.axis_index("tp")
    y, c = ep // 2, ep % 2
    parity = tp % 2
    mate = y * 2 + (1 - c)
    pair = tp + 1 - 2 * parity

    barrier = pltpu.get_barrier_semaphore()

    def greet_ep(i):
        pl.semaphore_signal(
            barrier, inc=1, device_id={"ep": lax.rem(ep + 1 + i, n_ep)}, device_id_type=MESH
        )

    def greet_tp(i):
        pl.semaphore_signal(
            barrier, inc=1, device_id={"tp": lax.rem(tp + 1 + i, n_tp)}, device_id_type=MESH
        )

    each(n_ep - 1, greet_ep)
    each(n_tp - 1, greet_tp)

    own_rows = pl.ds(pl.multiple_of(c * rows, rows), rows)
    mate_rows = pl.ds(pl.multiple_of((1 - c) * rows, rows), rows)
    own_copy = pltpu.make_async_copy(tok_hbm, tok_all.at[y, own_rows], tok_sem.at[0])
    own_copy.start()
    loads = [
        pltpu.make_async_copy(src, dst, w_sem.at[i])
        for i, (src, dst) in enumerate([
            (hg, vg), (hu, vu), (cg, wg), (cu, wu),
            (cd, wd.at[pl.ds(0, cold * ff)]), (hd, wd.at[pl.ds(cold * ff, hot * ff)]),
        ])
    ]
    for load in loads:
        load.start()

    ids = ids_ref[...]
    weights = weights_ref[...]
    scaled = ROUTE_SCALE * weights / jnp.sum(weights, axis=1, keepdims=True)
    slot = ids
    hot_coef = []
    for h in range(hot):
        slot = slot - (hot_ref[h] < ids).astype(jnp.int32)
    for h in range(hot):
        match = ids == hot_ref[h]
        slot = jnp.where(match, -1, slot)
        hot_coef.append(jnp.sum(jnp.where(match, scaled, 0.0), axis=1, keepdims=True))
    lane = lax.broadcasted_iota(jnp.int32, (rows, 128), 1)
    lane_slot = jnp.where(lane % 8 < cold, (lane // 8) * cold + lane % 8, -2)
    table = jnp.zeros((rows, 128), jnp.float32)
    for k in range(ids.shape[1]):
        table = table + jnp.where(lane_slot == slot[:, k:k + 1], scaled[:, k:k + 1], 0.0)
    coef_out[...] = table.T

    def coef_rows(e):
        return pl.ds(pl.multiple_of(8 * e, 8), 8)

    pl.semaphore_wait(barrier, n_ep - 1 + n_tp - 1)

    def remote(src, dst, sems, *at, **target):
        return pltpu.make_async_remote_copy(
            src_ref=src, dst_ref=dst, send_sem=sems.at[(0, *at)], recv_sem=sems.at[(1, *at)],
            device_id=target, device_id_type=MESH,
        )

    def block_rows(core, which, s):
        return pl.ds(pl.multiple_of(core * rows + which * half + s * run, run), run)

    def tok_y(j, s):
        there = lax.rem(y + 1 + j, ny)
        return remote(
            tok_hbm.at[pl.ds(pl.multiple_of(parity * half + s * run, run), run)],
            tok_all.at[y, block_rows(c, parity, s)],
            yt_sem, j, s, ep=there * 2 + c,
        )

    def source(j):
        return lax.rem(y + ny - 1 - j, ny)

    def landed_y(j, s):
        at = tok_all.at[source(j), block_rows(c, parity, s)]
        return remote(at, at, yt_sem, j, s, ep=lax.rem(y + 1 + j, ny) * 2 + c)

    def tok_z(j, s):
        at = tok_all.at[source(j), block_rows(c, parity, s)]
        return remote(at, at, zt_sem, j, s, tp=pair)

    def landed_z(j, s):
        at = tok_all.at[source(j), block_rows(c, 1 - parity, s)]
        return remote(at, at, zt_sem, j, s, tp=pair)

    def tok_c(j, q, s):
        which = parity if q == 0 else 1 - parity
        at = tok_all.at[source(j), block_rows(c, which, s)]
        return remote(at, at, ct_sem, j, q, s, ep=mate)

    def landed_c(j, q, s):
        which = parity if q == 0 else 1 - parity
        at = tok_all.at[source(j), block_rows(1 - c, which, s)]
        return remote(at, at, ct_sem, j, q, s, ep=mate)

    def coef_copy(i):
        e = lax.rem(ep + 1 + i, n_ep)
        return remote(
            coef_out.at[coef_rows(e)], coef_in.at[coef_rows(ep)], coef_sem, i, ep=e
        )

    def landed_coef(i):
        e = lax.rem(ep + n_ep - 1 - i, n_ep)
        return remote(
            coef_out.at[coef_rows(e)], coef_in.at[coef_rows(e)], coef_sem, i,
            ep=lax.rem(ep + 1 + i, n_ep),
        )

    block_copy = remote(tok_hbm, tok_all.at[y, own_rows], blk_sem, 0, ep=mate)
    block_landed = remote(tok_hbm, tok_all.at[y, mate_rows], blk_sem, 0, ep=mate)

    for s in range(SPLITS):
        each(ny - 1, lambda j: tok_y(j, s).start())
    block_copy.start()
    each(n_ep - 1, lambda i: coef_copy(i).start())
    coef_in[coef_rows(ep), :] = coef_out[coef_rows(ep), :]

    def pass_on(s):
        def step(j):
            landed_y(j, s).wait_recv()
            tok_z(j, s).start()
            tok_c(j, 0, s).start()
        each(ny - 1, step)

    def pass_across(s):
        def step(j):
            landed_z(j, s).wait_recv()
            tok_c(j, 1, s).start()
        each(ny - 1, step)

    def act(x, gate, up, coef):
        g = jnp.dot(x, gate, preferred_element_type=jnp.float32)
        u = jnp.dot(x, up, preferred_element_type=jnp.float32)
        return (g / (1.0 + jnp.exp(-g)) * u * coef).astype(jnp.bfloat16)

    def cold_coef(yy, e):
        one = coef_in[coef_rows(yy * 2), :].T[:, e:e + 1]
        two = coef_in[coef_rows(yy * 2 + 1), :].T[:, e:e + 1]
        return jnp.concatenate([one, two], axis=0)

    def cold_hidden(yy, e):
        hid[yy, :, e * ff:(e + 1) * ff] = act(tok_all[yy], wg[e], wu[e], cold_coef(yy, e))

    own_copy.wait()
    loads[0].wait()
    loads[1].wait()
    for h in range(hot):
        hot_hid[:, h * ff:(h + 1) * ff] = act(
            tok_all[y, own_rows], vg[h], vu[h], hot_coef[h]
        )
    pass_on(0)
    loads[2].wait()
    loads[3].wait()
    block_landed.wait_recv()
    each(n_ep - 1, lambda i: landed_coef(i).wait_recv())
    for e in range(cold):
        cold_hidden(y, e)
        pass_on(1 + e)
        pass_across(e)
    for s in range(1 + cold, SPLITS):
        pass_on(s)
    for s in range(cold, SPLITS):
        pass_across(s)
    for s in range(SPLITS):
        each(ny - 1, lambda j: landed_c(j, 0, s).wait_recv())
    for s in range(SPLITS):
        each(ny - 1, lambda j: landed_c(j, 1, s).wait_recv())

    def far_hidden(j):
        for e in range(cold):
            cold_hidden(lax.rem(y + 1 + j, ny), e)

    each(ny - 1, far_hidden)
    loads[4].wait()
    loads[5].wait()

    def columns(k):
        t = lax.rem(tp + 1 + k, n_tp)
        return pl.ds(pl.multiple_of(t * piece, 128), piece)

    def core_copy(j, k):
        return remote(core_out.at[j, k], core_in.at[j, k], core_sem, j, k, ep=mate)

    def y_copy(j, k):
        return remote(
            y_out.at[j, k], y_in.at[j, k], y_sem, j, k, ep=lax.rem(y + 1 + j, ny) * 2 + c
        )

    def z_copy(k):
        return remote(z_out.at[k], z_in.at[k], z_sem, k, tp=lax.rem(tp + 1 + k, n_tp))

    def project(j, k):
        yy = lax.rem(y + 1 + j, ny)
        part[...] = jnp.dot(
            hid[yy], wd[:cold * ff, columns(k)], preferred_element_type=jnp.float32
        )
        core_out[j, k] = part[mate_rows, :].astype(jnp.bfloat16)
        core_copy(j, k).start()

    def far(k):
        def step(j):
            project(j, k)
            keep = part[own_rows, :]
            core_copy(j, k).wait_recv()
            y_out[j, k] = (keep + core_in[j, k].astype(jnp.float32)).astype(jnp.bfloat16)
            y_copy(j, k).start()
        each(ny - 1, step)

    each(n_tp, far)

    def near(k):
        project(ny - 1, k)
        own_part[k] = part[own_rows, :] + jnp.dot(
            hot_hid[...], wd[cold * ff:, columns(k)], preferred_element_type=jnp.float32
        )

    each(n_tp, near)

    def total(k):
        core_copy(ny - 1, k).wait_recv()
        own_part[k] += core_in[ny - 1, k].astype(jnp.float32)

        def step(j):
            y_copy(j, k).wait_recv()
            own_part[k] += y_in[j, k].astype(jnp.float32)
        each(ny - 1, step)

    def hand_on(k):
        total(k)
        z_out[k] = own_part[k].astype(jnp.bfloat16)
        z_copy(k).start()

    each(n_tp - 1, hand_on)
    total(n_tp - 1)

    def collect(k):
        z_copy(k).wait_recv()
        own_part[n_tp - 1] += z_in[k].astype(jnp.float32)

    each(n_tp - 1, collect)
    out_ref[...] = own_part[n_tp - 1].astype(out_ref.dtype)

    block_copy.wait_send()
    each(n_ep - 1, lambda i: coef_copy(i).wait_send())
    for s in range(SPLITS):
        def sent(j):
            tok_y(j, s).wait_send()
            tok_z(j, s).wait_send()
            tok_c(j, 0, s).wait_send()
            tok_c(j, 1, s).wait_send()
        each(ny - 1, sent)

    def sums_sent(k):
        each(ny, lambda j: core_copy(j, k).wait_send())
        each(ny - 1, lambda j: y_copy(j, k).wait_send())

    each(n_tp, sums_sent)
    each(n_tp - 1, lambda k: z_copy(k).wait_send())


def per_device(
    n_ep, n_tp,
    tokens, expert_ids, route_weights, hot_list,
    cold_gate, cold_up, cold_down, hot_gate, hot_up, hot_down,
):
    rows, width = tokens.shape
    cold, _, ff = cold_gate.shape
    hot = hot_gate.shape[0]
    ny = n_ep // 2
    piece = width // n_tp
    padded = -(-piece // 128) * 128

    def flat(down):
        down = down.reshape(-1, n_tp, piece)
        if padded != piece:
            down = jnp.pad(down, ((0, 0), (0, 0), (0, padded - piece)))
        return down.reshape(-1, n_tp * padded)

    bf16, f32 = jnp.bfloat16, jnp.float32
    dma = pltpu.SemaphoreType.DMA
    vmem = pl.BlockSpec(memory_space=pltpu.VMEM)
    hbm = pl.BlockSpec(memory_space=pl.ANY)
    out = pl.pallas_call(
        functools.partial(layer_kernel, n_ep, n_tp),
        out_shape=jax.ShapeDtypeStruct((rows, padded), bf16),
        in_specs=[hbm, vmem, vmem, pl.BlockSpec(memory_space=pltpu.SMEM)] + [hbm] * 6,
        out_specs=vmem,
        scratch_shapes=[
            pltpu.VMEM((ny, 2 * rows, width), bf16),
            pltpu.VMEM((cold, width, ff), bf16),
            pltpu.VMEM((cold, width, ff), bf16),
            pltpu.VMEM((hot, width, ff), bf16),
            pltpu.VMEM((hot, width, ff), bf16),
            pltpu.VMEM(((cold + hot) * ff, n_tp * padded), bf16),
            pltpu.VMEM((ny, 2 * rows, cold * ff), bf16),
            pltpu.VMEM((rows, hot * ff), bf16),
            pltpu.VMEM((128, rows), f32),
            pltpu.VMEM((128, rows), f32),
            pltpu.VMEM((2 * rows, padded), f32),
            pltpu.VMEM((n_tp, rows, padded), f32),
            pltpu.VMEM((ny, n_tp, rows, padded), bf16),
            pltpu.VMEM((ny, n_tp, rows, padded), bf16),
            pltpu.VMEM((ny - 1, n_tp, rows, padded), bf16),
            pltpu.VMEM((ny - 1, n_tp, rows, padded), bf16),
            pltpu.VMEM((n_tp - 1, rows, padded), bf16),
            pltpu.VMEM((n_tp - 1, rows, padded), bf16),
            dma((6,)),
            dma((1,)),
            dma((2, n_ep - 1)),
            dma((2, 1)),
            dma((2, ny - 1, SPLITS)),
            dma((2, ny - 1, SPLITS)),
            dma((2, ny - 1, 2, SPLITS)),
            dma((2, ny, n_tp)),
            dma((2, ny - 1, n_tp)),
            dma((2, n_tp - 1)),
        ],
        compiler_params=pltpu.CompilerParams(
            collective_id=0, has_side_effects=True, vmem_limit_bytes=63 * 1024 * 1024
        ),
        cost_estimate=pl.CostEstimate(
            flops=2 * rows * (n_ep * cold + hot) * 3 * width * ff,
            bytes_accessed=2 * 3 * (cold + hot) * width * ff,
            transcendentals=rows * (n_ep * cold + hot) * ff,
        ),
    )(
        tokens, expert_ids, route_weights, hot_list,
        cold_gate, cold_up, flat(cold_down), hot_gate, hot_up, flat(hot_down),
    )
    return out[:, :piece]


def solution(mesh):
    placed = (
        P(("groups", "ep"), None),
        P(("groups", "ep"), None),
        P(("groups", "ep"), None),
        P("groups"),
        P("ep", None, "tp"),
        P("ep", None, "tp"),
        P("ep", "tp", None),
        P(None, None, "tp"),
        P(None, None, "tp"),
        P(None, "tp", None),
    )
    return jax.shard_map(
        functools.partial(per_device, mesh.shape["ep"], mesh.shape["tp"]),
        mesh=mesh, in_specs=placed, out_specs=P(("groups", "ep"), "tp"), check_vma=False,
    )
```

```python
import functools

import jax
import jax.numpy as jnp
from jax import lax
from jax.experimental import pallas as pl
from jax.experimental.pallas import tpu as pltpu
from jax.sharding import PartitionSpec as P

ROUTE_SCALE = 2.5
MESH = pl.DeviceIdType.MESH
SPLITS = 2
PARTS = 2


def each(count, step):
    if count <= 4:
        for index in range(count):
            step(index)
    else:
        pl.loop(0, count)(step)


def layer_kernel(
    n_ep, n_tp,
    tok_hbm, ids_ref, weights_ref, hot_ref, cg, cu, cd, hg, hu, hd,
    out_ref,
    tok_all, wg, wu, vg, vu, wd, hid, hot_hid, coef_out, coef_in, part, own_part,
    core_out, core_in, y_out, y_in, z_out, z_in,
    w_sem, tok_sem, coef_sem, blk_sem, yt_sem, zt_sem, ct_sem, core_sem, y_sem, z_sem,
):
    rows, width = tok_hbm.shape
    cold, _, ff = wg.shape
    hot = vg.shape[0]
    piece = out_ref.shape[1]
    ny = n_ep // 2
    half = rows // 2
    run = half // SPLITS
    ep, tp = lax.axis_index("ep"), lax.axis_index("tp")
    y, c = ep // 2, ep % 2
    parity = tp % 2
    mate = y * 2 + (1 - c)
    pair = tp + 1 - 2 * parity

    barrier = pltpu.get_barrier_semaphore()

    def greet_ep(i):
        pl.semaphore_signal(
            barrier, inc=1, device_id={"ep": lax.rem(ep + 1 + i, n_ep)}, device_id_type=MESH
        )

    def greet_tp(i):
        pl.semaphore_signal(
            barrier, inc=1, device_id={"tp": lax.rem(tp + 1 + i, n_tp)}, device_id_type=MESH
        )

    each(n_ep - 1, greet_ep)
    each(n_tp - 1, greet_tp)

    own_rows = pl.ds(pl.multiple_of(c * rows, rows), rows)
    mate_rows = pl.ds(pl.multiple_of((1 - c) * rows, rows), rows)
    own_copy = pltpu.make_async_copy(tok_hbm, tok_all.at[y, own_rows], tok_sem.at[0])
    own_copy.start()
    loads = [
        pltpu.make_async_copy(src, dst, w_sem.at[i])
        for i, (src, dst) in enumerate([
            (hg, vg), (hu, vu), (cg, wg), (cu, wu),
            (cd, wd.at[pl.ds(0, cold * ff)]), (hd, wd.at[pl.ds(cold * ff, hot * ff)]),
        ])
    ]
    for load in loads:
        load.start()

    ids = ids_ref[...].astype(jnp.float32).T.astype(jnp.int32)
    weights = weights_ref[...].T
    scaled = ROUTE_SCALE * weights / jnp.sum(weights, axis=1, keepdims=True)
    slot = ids
    hot_coef = []
    for h in range(hot):
        slot = slot - (hot_ref[h] < ids).astype(jnp.int32)
    for h in range(hot):
        match = ids == hot_ref[h]
        slot = jnp.where(match, -1, slot)
        hot_coef.append(jnp.sum(jnp.where(match, scaled, 0.0), axis=1, keepdims=True))
    lane = lax.broadcasted_iota(jnp.int32, (rows, 128), 1)
    lane_slot = jnp.where(lane % 8 < cold, (lane // 8) * cold + lane % 8, -2)
    table = jnp.zeros((rows, 128), jnp.float32)
    for k in range(ids.shape[1]):
        table = table + jnp.where(lane_slot == slot[:, k:k + 1], scaled[:, k:k + 1], 0.0)
    coef_out[...] = table.T

    def coef_rows(e):
        return pl.ds(pl.multiple_of(8 * e, 8), 8)

    pl.semaphore_wait(barrier, n_ep - 1 + n_tp - 1)

    def remote(src, dst, sems, *at, **target):
        return pltpu.make_async_remote_copy(
            src_ref=src, dst_ref=dst, send_sem=sems.at[(0, *at)], recv_sem=sems.at[(1, *at)],
            device_id=target, device_id_type=MESH,
        )

    def block_rows(core, which, s):
        return pl.ds(pl.multiple_of(core * rows + which * half + s * run, run), run)

    def tok_y(j, s):
        there = lax.rem(y + 1 + j, ny)
        return remote(
            tok_hbm.at[pl.ds(pl.multiple_of(parity * half + s * run, run), run)],
            tok_all.at[y, block_rows(c, parity, s)],
            yt_sem, j, s, ep=there * 2 + c,
        )

    def source(j):
        return lax.rem(y + ny - 1 - j, ny)

    def landed_y(j, s):
        at = tok_all.at[source(j), block_rows(c, parity, s)]
        return remote(at, at, yt_sem, j, s, ep=lax.rem(y + 1 + j, ny) * 2 + c)

    def tok_z(j, s):
        at = tok_all.at[source(j), block_rows(c, parity, s)]
        return remote(at, at, zt_sem, j, s, tp=pair)

    def landed_z(j, s):
        at = tok_all.at[source(j), block_rows(c, 1 - parity, s)]
        return remote(at, at, zt_sem, j, s, tp=pair)

    def tok_c(j, q, s):
        which = parity if q == 0 else 1 - parity
        at = tok_all.at[source(j), block_rows(c, which, s)]
        return remote(at, at, ct_sem, j, q, s, ep=mate)

    def landed_c(j, q, s):
        which = parity if q == 0 else 1 - parity
        at = tok_all.at[source(j), block_rows(1 - c, which, s)]
        return remote(at, at, ct_sem, j, q, s, ep=mate)

    def coef_copy(i):
        e = lax.rem(ep + 1 + i, n_ep)
        return remote(
            coef_out.at[coef_rows(e)], coef_in.at[coef_rows(ep)], coef_sem, i, ep=e
        )

    def landed_coef(i):
        e = lax.rem(ep + n_ep - 1 - i, n_ep)
        return remote(
            coef_out.at[coef_rows(e)], coef_in.at[coef_rows(e)], coef_sem, i,
            ep=lax.rem(ep + 1 + i, n_ep),
        )

    block_copy = remote(tok_hbm, tok_all.at[y, own_rows], blk_sem, 0, ep=mate)
    block_landed = remote(tok_hbm, tok_all.at[y, mate_rows], blk_sem, 0, ep=mate)

    for s in range(SPLITS):
        each(ny - 1, lambda j: tok_y(j, s).start())
    block_copy.start()
    each(n_ep - 1, lambda i: coef_copy(i).start())
    coef_in[coef_rows(ep), :] = coef_out[coef_rows(ep), :]

    def pass_on(s):
        def step(j):
            landed_y(j, s).wait_recv()
            tok_z(j, s).start()
            tok_c(j, 0, s).start()
        each(ny - 1, step)

    def pass_across(s):
        def step(j):
            landed_z(j, s).wait_recv()
            tok_c(j, 1, s).start()
        each(ny - 1, step)

    def act(x, gate, up, coef):
        g = jnp.dot(x, gate, preferred_element_type=jnp.float32)
        u = jnp.dot(x, up, preferred_element_type=jnp.float32)
        return (g / (1.0 + jnp.exp(-g)) * u * coef).astype(jnp.bfloat16)

    def cold_coef(yy, e):
        one = coef_in[coef_rows(yy * 2), :].T[:, e:e + 1]
        two = coef_in[coef_rows(yy * 2 + 1), :].T[:, e:e + 1]
        return jnp.concatenate([one, two], axis=0)

    def cold_hidden(yy, e):
        hid[yy, :, e * ff:(e + 1) * ff] = act(tok_all[yy], wg[e], wu[e], cold_coef(yy, e))

    own_copy.wait()
    loads[0].wait()
    loads[1].wait()
    for h in range(hot):
        hot_hid[:, h * ff:(h + 1) * ff] = act(
            tok_all[y, own_rows], vg[h], vu[h], hot_coef[h]
        )
    pass_on(0)
    loads[2].wait()
    loads[3].wait()
    block_landed.wait_recv()
    each(n_ep - 1, lambda i: landed_coef(i).wait_recv())
    for e in range(cold):
        cold_hidden(y, e)
        if 1 + e < SPLITS:
            pass_on(1 + e)
        if e < SPLITS:
            pass_across(e)
    for s in range(1 + cold, SPLITS):
        pass_on(s)
    for s in range(cold, SPLITS):
        pass_across(s)
    for s in range(SPLITS):
        each(ny - 1, lambda j: landed_c(j, 0, s).wait_recv())
    for s in range(SPLITS):
        each(ny - 1, lambda j: landed_c(j, 1, s).wait_recv())

    def far_hidden(j):
        for e in range(cold):
            cold_hidden(lax.rem(y + 1 + j, ny), e)

    each(ny - 1, far_hidden)
    loads[4].wait()
    loads[5].wait()

    def columns(k):
        t = lax.rem(tp + 1 + k, n_tp)
        return pl.ds(pl.multiple_of(t * piece, 128), piece)

    span = rows // PARTS

    def cut(r):
        return pl.ds(r * span, span)

    def core_copy(j, k, r):
        return remote(
            core_out.at[j, k, cut(r)], core_in.at[j, k, cut(r)], core_sem, j, k, r, ep=mate
        )

    def y_copy(j, k, r):
        return remote(
            y_out.at[j, k, cut(r)], y_in.at[j, k, cut(r)], y_sem, j, k, r,
            ep=lax.rem(y + 1 + j, ny) * 2 + c,
        )

    def z_copy(k, r):
        return remote(
            z_out.at[k, cut(r)], z_in.at[k, cut(r)], z_sem, k, r, tp=lax.rem(tp + 1 + k, n_tp)
        )

    def project(j, k):
        yy = lax.rem(y + 1 + j, ny)
        part[...] = jnp.dot(
            hid[yy], wd[:cold * ff, columns(k)], preferred_element_type=jnp.float32
        )
        core_out[j, k] = part[mate_rows, :].astype(jnp.bfloat16)
        for r in range(PARTS):
            core_copy(j, k, r).start()

    def far(k):
        def step(j):
            project(j, k)
            for r in range(PARTS):
                keep = part[pl.ds(pl.multiple_of(c * rows + r * span, span), span), :]
                core_copy(j, k, r).wait_recv()
                y_out[j, k, cut(r)] = (
                    keep + core_in[j, k, cut(r)].astype(jnp.float32)
                ).astype(jnp.bfloat16)
                y_copy(j, k, r).start()
        each(ny - 1, step)

    each(n_tp, far)

    def near(k):
        project(ny - 1, k)
        own_part[k] = part[own_rows, :] + jnp.dot(
            hot_hid[...], wd[cold * ff:, columns(k)], preferred_element_type=jnp.float32
        )

    each(n_tp, near)

    def total(k, r):
        core_copy(ny - 1, k, r).wait_recv()
        own_part[k, cut(r)] += core_in[ny - 1, k, cut(r)].astype(jnp.float32)

        def step(j):
            y_copy(j, k, r).wait_recv()
            own_part[k, cut(r)] += y_in[j, k, cut(r)].astype(jnp.float32)
        each(ny - 1, step)

    def hand_on(k):
        for r in range(PARTS):
            total(k, r)
            z_out[k, cut(r)] = own_part[k, cut(r)].astype(jnp.bfloat16)
            z_copy(k, r).start()

    each(n_tp - 1, hand_on)
    for r in range(PARTS):
        total(n_tp - 1, r)

    def collect(k):
        for r in range(PARTS):
            z_copy(k, r).wait_recv()
            own_part[n_tp - 1, cut(r)] += z_in[k, cut(r)].astype(jnp.float32)

    each(n_tp - 1, collect)
    out_ref[...] = own_part[n_tp - 1].astype(out_ref.dtype)

    block_copy.wait_send()
    each(n_ep - 1, lambda i: coef_copy(i).wait_send())
    for s in range(SPLITS):
        def sent(j):
            tok_y(j, s).wait_send()
            tok_z(j, s).wait_send()
            tok_c(j, 0, s).wait_send()
            tok_c(j, 1, s).wait_send()
        each(ny - 1, sent)

    def sums_sent(k):
        for r in range(PARTS):
            each(ny, lambda j: core_copy(j, k, r).wait_send())
            each(ny - 1, lambda j: y_copy(j, k, r).wait_send())

    each(n_tp, sums_sent)
    for r in range(PARTS):
        each(n_tp - 1, lambda k: z_copy(k, r).wait_send())


def per_device(
    n_ep, n_tp,
    tokens, expert_ids, route_weights, hot_list,
    cold_gate, cold_up, cold_down, hot_gate, hot_up, hot_down,
):
    rows, width = tokens.shape
    cold, _, ff = cold_gate.shape
    hot = hot_gate.shape[0]
    ny = n_ep // 2
    piece = width // n_tp
    padded = -(-piece // 128) * 128

    def flat(down):
        down = down.reshape(-1, n_tp, piece)
        if padded != piece:
            down = jnp.pad(down, ((0, 0), (0, 0), (0, padded - piece)))
        return down.reshape(-1, n_tp * padded)

    bf16, f32 = jnp.bfloat16, jnp.float32
    dma = pltpu.SemaphoreType.DMA
    vmem = pl.BlockSpec(memory_space=pltpu.VMEM)
    hbm = pl.BlockSpec(memory_space=pl.ANY)
    out = pl.pallas_call(
        functools.partial(layer_kernel, n_ep, n_tp),
        out_shape=jax.ShapeDtypeStruct((rows, padded), bf16),
        in_specs=[hbm, vmem, vmem, pl.BlockSpec(memory_space=pltpu.SMEM)] + [hbm] * 6,
        out_specs=vmem,
        scratch_shapes=[
            pltpu.VMEM((ny, 2 * rows, width), bf16),
            pltpu.VMEM((cold, width, ff), bf16),
            pltpu.VMEM((cold, width, ff), bf16),
            pltpu.VMEM((hot, width, ff), bf16),
            pltpu.VMEM((hot, width, ff), bf16),
            pltpu.VMEM(((cold + hot) * ff, n_tp * padded), bf16),
            pltpu.VMEM((ny, 2 * rows, cold * ff), bf16),
            pltpu.VMEM((rows, hot * ff), bf16),
            pltpu.VMEM((128, rows), f32),
            pltpu.VMEM((128, rows), f32),
            pltpu.VMEM((2 * rows, padded), f32),
            pltpu.VMEM((n_tp, rows, padded), f32),
            pltpu.VMEM((ny, n_tp, rows, padded), bf16),
            pltpu.VMEM((ny, n_tp, rows, padded), bf16),
            pltpu.VMEM((ny - 1, n_tp, rows, padded), bf16),
            pltpu.VMEM((ny - 1, n_tp, rows, padded), bf16),
            pltpu.VMEM((n_tp - 1, rows, padded), bf16),
            pltpu.VMEM((n_tp - 1, rows, padded), bf16),
            dma((6,)),
            dma((1,)),
            dma((2, n_ep - 1)),
            dma((2, 1)),
            dma((2, ny - 1, SPLITS)),
            dma((2, ny - 1, SPLITS)),
            dma((2, ny - 1, 2, SPLITS)),
            dma((2, ny, n_tp, PARTS)),
            dma((2, ny - 1, n_tp, PARTS)),
            dma((2, n_tp - 1, PARTS)),
        ],
        compiler_params=pltpu.CompilerParams(
            collective_id=0, has_side_effects=True, vmem_limit_bytes=63 * 1024 * 1024
        ),
        cost_estimate=pl.CostEstimate(
            flops=2 * rows * (n_ep * cold + hot) * 3 * width * ff,
            bytes_accessed=2 * 3 * (cold + hot) * width * ff,
            transcendentals=rows * (n_ep * cold + hot) * ff,
        ),
    )(
        tokens, expert_ids.T, route_weights.T, hot_list,
        cold_gate, cold_up, flat(cold_down), hot_gate, hot_up, flat(hot_down),
    )
    return out[:, :piece]


def solution(mesh):
    placed = (
        P(("groups", "ep"), None),
        P(("groups", "ep"), None),
        P(("groups", "ep"), None),
        P("groups"),
        P("ep", None, "tp"),
        P("ep", None, "tp"),
        P("ep", "tp", None),
        P(None, None, "tp"),
        P(None, None, "tp"),
        P(None, "tp", None),
    )
    return jax.shard_map(
        functools.partial(per_device, mesh.shape["ep"], mesh.shape["tp"]),
        mesh=mesh, in_specs=placed, out_specs=P(("groups", "ep"), "tp"), check_vma=False,
    )
```

```python
import functools

import jax
import jax.numpy as jnp
from jax import lax
from jax.experimental import pallas as pl
from jax.experimental.pallas import tpu as pltpu
from jax.sharding import PartitionSpec as P

ROUTE_SCALE = 2.5
MESH = pl.DeviceIdType.MESH
SPLITS = 4
PARTS = 2
FLIGHT = 2


def each(count, step):
    if count <= 4:
        for index in range(count):
            step(index)
    else:
        pl.loop(0, count)(step)


def layer_kernel(
    n_ep, n_tp,
    tok_hbm, ids_ref, weights_ref, hot_ref, cg, cu, cd, hg, hu, hd,
    out_ref,
    tok_all, wg, wu, vg, vu, wd, hid, hot_hid, coef_out, coef_in, part, own_part,
    core_out, core_in, y_out, y_in, z_out, z_in,
    w_sem, tok_sem, coef_sem, blk_sem, yt_sem, zt_sem, ct_sem, core_sem, y_sem, z_sem,
):
    rows, width = tok_hbm.shape
    cold, _, ff = wg.shape
    hot = vg.shape[0]
    piece = out_ref.shape[1]
    ny = n_ep // 2
    half = rows // 2
    run = half // SPLITS
    ep, tp = lax.axis_index("ep"), lax.axis_index("tp")
    y, c = ep // 2, ep % 2
    parity = tp % 2
    mate = y * 2 + (1 - c)
    pair = tp + 1 - 2 * parity

    barrier = pltpu.get_barrier_semaphore()

    def greet_ep(i):
        pl.semaphore_signal(
            barrier, inc=1, device_id={"ep": lax.rem(ep + 1 + i, n_ep)}, device_id_type=MESH
        )

    def greet_tp(i):
        pl.semaphore_signal(
            barrier, inc=1, device_id={"tp": lax.rem(tp + 1 + i, n_tp)}, device_id_type=MESH
        )

    each(n_ep - 1, greet_ep)
    each(n_tp - 1, greet_tp)

    own_rows = pl.ds(pl.multiple_of(c * rows, rows), rows)
    mate_rows = pl.ds(pl.multiple_of((1 - c) * rows, rows), rows)
    own_copy = pltpu.make_async_copy(tok_hbm, tok_all.at[y, own_rows], tok_sem.at[0])
    own_copy.start()
    loads = [
        pltpu.make_async_copy(src, dst, w_sem.at[i])
        for i, (src, dst) in enumerate([
            (hg, vg), (hu, vu), (cg, wg), (cu, wu),
            (cd, wd.at[pl.ds(0, cold * ff)]), (hd, wd.at[pl.ds(cold * ff, hot * ff)]),
        ])
    ]
    for load in loads:
        load.start()

    ids = ids_ref[...].astype(jnp.float32).T.astype(jnp.int32)
    weights = weights_ref[...].T
    scaled = ROUTE_SCALE * weights / jnp.sum(weights, axis=1, keepdims=True)
    slot = ids
    hot_coef = []
    for h in range(hot):
        slot = slot - (hot_ref[h] < ids).astype(jnp.int32)
    for h in range(hot):
        match = ids == hot_ref[h]
        slot = jnp.where(match, -1, slot)
        hot_coef.append(jnp.sum(jnp.where(match, scaled, 0.0), axis=1, keepdims=True))
    lane = lax.broadcasted_iota(jnp.int32, (rows, 128), 1)
    lane_slot = jnp.where(lane % 8 < cold, (lane // 8) * cold + lane % 8, -2)
    table = jnp.zeros((rows, 128), jnp.float32)
    for k in range(ids.shape[1]):
        table = table + jnp.where(lane_slot == slot[:, k:k + 1], scaled[:, k:k + 1], 0.0)
    coef_out[...] = table.T

    def coef_rows(e):
        return pl.ds(pl.multiple_of(8 * e, 8), 8)

    pl.semaphore_wait(barrier, n_ep - 1 + n_tp - 1)

    def remote(src, dst, sems, *at, **target):
        return pltpu.make_async_remote_copy(
            src_ref=src, dst_ref=dst, send_sem=sems.at[(0, *at)], recv_sem=sems.at[(1, *at)],
            device_id=target, device_id_type=MESH,
        )

    def block_rows(core, which, s):
        return pl.ds(pl.multiple_of(core * rows + which * half + s * run, run), run)

    def tok_y(j, s):
        there = lax.rem(y + 1 + j, ny)
        return remote(
            tok_hbm.at[pl.ds(pl.multiple_of(parity * half + s * run, run), run)],
            tok_all.at[y, block_rows(c, parity, s)],
            yt_sem, j, s, ep=there * 2 + c,
        )

    def source(j):
        return lax.rem(y + ny - 1 - j, ny)

    def landed_y(j, s):
        at = tok_all.at[source(j), block_rows(c, parity, s)]
        return remote(at, at, yt_sem, j, s, ep=lax.rem(y + 1 + j, ny) * 2 + c)

    def tok_z(j, s):
        at = tok_all.at[source(j), block_rows(c, parity, s)]
        return remote(at, at, zt_sem, j, s, tp=pair)

    def landed_z(j, s):
        at = tok_all.at[source(j), block_rows(c, 1 - parity, s)]
        return remote(at, at, zt_sem, j, s, tp=pair)

    def tok_c(j, q, s):
        which = parity if q == 0 else 1 - parity
        at = tok_all.at[source(j), block_rows(c, which, s)]
        return remote(at, at, ct_sem, j, q, s, ep=mate)

    def landed_c(j, q, s):
        which = parity if q == 0 else 1 - parity
        at = tok_all.at[source(j), block_rows(1 - c, which, s)]
        return remote(at, at, ct_sem, j, q, s, ep=mate)

    def coef_copy(i):
        e = lax.rem(ep + 1 + i, n_ep)
        return remote(
            coef_out.at[coef_rows(e)], coef_in.at[coef_rows(ep)], coef_sem, i, ep=e
        )

    def landed_coef(i):
        e = lax.rem(ep + n_ep - 1 - i, n_ep)
        return remote(
            coef_out.at[coef_rows(e)], coef_in.at[coef_rows(e)], coef_sem, i,
            ep=lax.rem(ep + 1 + i, n_ep),
        )

    block_copy = remote(tok_hbm, tok_all.at[y, own_rows], blk_sem, 0, ep=mate)
    block_landed = remote(tok_hbm, tok_all.at[y, mate_rows], blk_sem, 0, ep=mate)

    for s in range(FLIGHT):
        each(ny - 1, lambda j: tok_y(j, s).start())
    block_copy.start()
    each(n_ep - 1, lambda i: coef_copy(i).start())
    coef_in[coef_rows(ep), :] = coef_out[coef_rows(ep), :]

    def pass_on(s):
        def step(j):
            if s + FLIGHT < SPLITS:
                tok_y(j, s).wait_send()
                tok_y(j, s + FLIGHT).start()
            landed_y(j, s).wait_recv()
            tok_z(j, s).start()
            tok_c(j, 0, s).start()
        each(ny - 1, step)

    def pass_across(s):
        def step(j):
            landed_z(j, s).wait_recv()
            tok_c(j, 1, s).start()
        each(ny - 1, step)

    def act(x, gate, up, coef):
        g = jnp.dot(x, gate, preferred_element_type=jnp.float32)
        u = jnp.dot(x, up, preferred_element_type=jnp.float32)
        return (g / (1.0 + jnp.exp(-g)) * u * coef).astype(jnp.bfloat16)

    def cold_coef(yy, e):
        one = coef_in[coef_rows(yy * 2), :].T[:, e:e + 1]
        two = coef_in[coef_rows(yy * 2 + 1), :].T[:, e:e + 1]
        return jnp.concatenate([one, two], axis=0)

    def cold_hidden(yy, e):
        hid[yy, :, e * ff:(e + 1) * ff] = act(tok_all[yy], wg[e], wu[e], cold_coef(yy, e))

    own_copy.wait()
    loads[0].wait()
    loads[1].wait()
    for h in range(hot):
        hot_hid[:, h * ff:(h + 1) * ff] = act(
            tok_all[y, own_rows], vg[h], vu[h], hot_coef[h]
        )
        if h < 2:
            pass_on(h)
    loads[2].wait()
    loads[3].wait()
    block_landed.wait_recv()
    each(n_ep - 1, lambda i: landed_coef(i).wait_recv())
    begun = min(hot, 2)
    for e in range(cold):
        cold_hidden(y, e)
        if begun + e < SPLITS:
            pass_on(begun + e)
        if e < SPLITS:
            pass_across(e)
    for s in range(begun + cold, SPLITS):
        pass_on(s)
    for s in range(cold, SPLITS):
        pass_across(s)
    for s in range(SPLITS):
        each(ny - 1, lambda j: landed_c(j, 0, s).wait_recv())
    for s in range(SPLITS):
        each(ny - 1, lambda j: landed_c(j, 1, s).wait_recv())

    def far_hidden(j):
        for e in range(cold):
            cold_hidden(lax.rem(y + 1 + j, ny), e)

    each(ny - 1, far_hidden)
    loads[4].wait()
    loads[5].wait()

    def columns(k):
        t = lax.rem(tp + 1 + k, n_tp)
        return pl.ds(pl.multiple_of(t * piece, 128), piece)

    span = rows // PARTS

    def cut(r):
        return pl.ds(r * span, span)

    def core_copy(j, k, r):
        return remote(
            core_out.at[j, k, cut(r)], core_in.at[j, k, cut(r)], core_sem, j, k, r, ep=mate
        )

    def y_copy(j, k, r):
        return remote(
            y_out.at[j, k, cut(r)], y_in.at[j, k, cut(r)], y_sem, j, k, r,
            ep=lax.rem(y + 1 + j, ny) * 2 + c,
        )

    def z_copy(k, r):
        return remote(
            z_out.at[k, cut(r)], z_in.at[k, cut(r)], z_sem, k, r, tp=lax.rem(tp + 1 + k, n_tp)
        )

    def project(j, k):
        yy = lax.rem(y + 1 + j, ny)
        part[...] = jnp.dot(
            hid[yy], wd[:cold * ff, columns(k)], preferred_element_type=jnp.float32
        )
        core_out[j, k] = part[mate_rows, :].astype(jnp.bfloat16)
        for r in range(PARTS):
            core_copy(j, k, r).start()

    def far(k):
        def step(j):
            project(j, k)
            for r in range(PARTS):
                keep = part[pl.ds(pl.multiple_of(c * rows + r * span, span), span), :]
                core_copy(j, k, r).wait_recv()
                y_out[j, k, cut(r)] = (
                    keep + core_in[j, k, cut(r)].astype(jnp.float32)
                ).astype(jnp.bfloat16)
        each(ny - 1, step)

    def send_y(k, r):
        def step(j):
            if k > 0:
                y_copy(j, k - 1, r).wait_send()
            y_copy(j, k, r).start()
        each(ny - 1, step)

    def near(k):
        project(ny - 1, k)
        own_part[k] = part[own_rows, :] + jnp.dot(
            hot_hid[...], wd[cold * ff:, columns(k)], preferred_element_type=jnp.float32
        )

    def total(k, r):
        core_copy(ny - 1, k, r).wait_recv()
        own_part[k, cut(r)] += core_in[ny - 1, k, cut(r)].astype(jnp.float32)

        def step(j):
            y_copy(j, k, r).wait_recv()
            own_part[k, cut(r)] += y_in[j, k, cut(r)].astype(jnp.float32)
        each(ny - 1, step)

    def hand_on(k, r):
        total(k, r)
        z_out[k, cut(r)] = own_part[k, cut(r)].astype(jnp.bfloat16)
        z_copy(k, r).start()

    for k in range(n_tp):
        far(k)
        send_y(k, 0)
        if k == 0:
            for r in range(1, PARTS):
                send_y(k, r)
        near(k)
        if k > 0:
            hand_on(k - 1, 0)
            for r in range(1, PARTS):
                send_y(k, r)
                hand_on(k - 1, r)
    for r in range(PARTS):
        total(n_tp - 1, r)

    def collect(k):
        for r in range(PARTS):
            z_copy(k, r).wait_recv()
            own_part[n_tp - 1, cut(r)] += z_in[k, cut(r)].astype(jnp.float32)

    each(n_tp - 1, collect)
    out_ref[...] = own_part[n_tp - 1].astype(out_ref.dtype)

    block_copy.wait_send()
    each(n_ep - 1, lambda i: coef_copy(i).wait_send())
    for s in range(SPLITS):
        def sent(j):
            if s + FLIGHT >= SPLITS:
                tok_y(j, s).wait_send()
            tok_z(j, s).wait_send()
            tok_c(j, 0, s).wait_send()
            tok_c(j, 1, s).wait_send()
        each(ny - 1, sent)

    def sums_sent(k):
        for r in range(PARTS):
            each(ny, lambda j: core_copy(j, k, r).wait_send())

    each(n_tp, sums_sent)
    for r in range(PARTS):
        each(ny - 1, lambda j: y_copy(j, n_tp - 1, r).wait_send())
        each(n_tp - 1, lambda k: z_copy(k, r).wait_send())


def per_device(
    n_ep, n_tp,
    tokens, expert_ids, route_weights, hot_list,
    cold_gate, cold_up, cold_down, hot_gate, hot_up, hot_down,
):
    rows, width = tokens.shape
    cold, _, ff = cold_gate.shape
    hot = hot_gate.shape[0]
    ny = n_ep // 2
    piece = width // n_tp
    padded = -(-piece // 128) * 128

    def flat(down):
        down = down.reshape(-1, n_tp, piece)
        if padded != piece:
            down = jnp.pad(down, ((0, 0), (0, 0), (0, padded - piece)))
        return down.reshape(-1, n_tp * padded)

    bf16, f32 = jnp.bfloat16, jnp.float32
    dma = pltpu.SemaphoreType.DMA
    vmem = pl.BlockSpec(memory_space=pltpu.VMEM)
    hbm = pl.BlockSpec(memory_space=pl.ANY)
    out = pl.pallas_call(
        functools.partial(layer_kernel, n_ep, n_tp),
        out_shape=jax.ShapeDtypeStruct((rows, padded), bf16),
        in_specs=[hbm, vmem, vmem, pl.BlockSpec(memory_space=pltpu.SMEM)] + [hbm] * 6,
        out_specs=vmem,
        scratch_shapes=[
            pltpu.VMEM((ny, 2 * rows, width), bf16),
            pltpu.VMEM((cold, width, ff), bf16),
            pltpu.VMEM((cold, width, ff), bf16),
            pltpu.VMEM((hot, width, ff), bf16),
            pltpu.VMEM((hot, width, ff), bf16),
            pltpu.VMEM(((cold + hot) * ff, n_tp * padded), bf16),
            pltpu.VMEM((ny, 2 * rows, cold * ff), bf16),
            pltpu.VMEM((rows, hot * ff), bf16),
            pltpu.VMEM((128, rows), f32),
            pltpu.VMEM((128, rows), f32),
            pltpu.VMEM((2 * rows, padded), f32),
            pltpu.VMEM((n_tp, rows, padded), f32),
            pltpu.VMEM((ny, n_tp, rows, padded), bf16),
            pltpu.VMEM((ny, n_tp, rows, padded), bf16),
            pltpu.VMEM((ny - 1, n_tp, rows, padded), bf16),
            pltpu.VMEM((ny - 1, n_tp, rows, padded), bf16),
            pltpu.VMEM((n_tp - 1, rows, padded), bf16),
            pltpu.VMEM((n_tp - 1, rows, padded), bf16),
            dma((6,)),
            dma((1,)),
            dma((2, n_ep - 1)),
            dma((2, 1)),
            dma((2, ny - 1, SPLITS)),
            dma((2, ny - 1, SPLITS)),
            dma((2, ny - 1, 2, SPLITS)),
            dma((2, ny, n_tp, PARTS)),
            dma((2, ny - 1, n_tp, PARTS)),
            dma((2, n_tp - 1, PARTS)),
        ],
        compiler_params=pltpu.CompilerParams(
            collective_id=0, has_side_effects=True, vmem_limit_bytes=63 * 1024 * 1024
        ),
        cost_estimate=pl.CostEstimate(
            flops=2 * rows * (n_ep * cold + hot) * 3 * width * ff,
            bytes_accessed=2 * 3 * (cold + hot) * width * ff,
            transcendentals=rows * (n_ep * cold + hot) * ff,
        ),
    )(
        tokens, expert_ids.T, route_weights.T, hot_list,
        cold_gate, cold_up, flat(cold_down), hot_gate, hot_up, flat(hot_down),
    )
    return out[:, :piece]


def solution(mesh):
    placed = (
        P(("groups", "ep"), None),
        P(("groups", "ep"), None),
        P(("groups", "ep"), None),
        P("groups"),
        P("ep", None, "tp"),
        P("ep", None, "tp"),
        P("ep", "tp", None),
        P(None, None, "tp"),
        P(None, None, "tp"),
        P(None, "tp", None),
    )
    return jax.shard_map(
        functools.partial(per_device, mesh.shape["ep"], mesh.shape["tp"]),
        mesh=mesh, in_specs=placed, out_specs=P(("groups", "ep"), "tp"), check_vma=False,
    )
```

```python
import functools

import jax
import jax.numpy as jnp
from jax import lax
from jax.experimental import pallas as pl
from jax.experimental.pallas import tpu as pltpu
from jax.sharding import PartitionSpec as P

ROUTE_SCALE = 2.5
MESH = pl.DeviceIdType.MESH
SPLITS = 4
PARTS = 2
FLIGHT = 2


def each(count, step):
    if count <= 4:
        for index in range(count):
            step(index)
    else:
        pl.loop(0, count)(step)


def layer_kernel(
    n_ep, n_tp,
    tok_hbm, ids_ref, weights_ref, hot_ref, cg, cu, cd, hg, hu, hd,
    out_ref,
    tok_all, wg, wu, vg, vu, wd, hid, hot_hid, coef_out, coef_in, part, own_part,
    core_out, core_in, y_out, y_in, z_out, z_in,
    w_sem, tok_sem, coef_sem, blk_sem, yt_sem, zt_sem, ct_sem, core_sem, y_sem, z_sem,
):
    rows, width = tok_hbm.shape
    cold, _, ff = wg.shape
    hot = vg.shape[0]
    piece = out_ref.shape[1]
    ny = n_ep // 2
    half = rows // 2
    run = half // SPLITS
    ep, tp = lax.axis_index("ep"), lax.axis_index("tp")
    y, c = ep // 2, ep % 2
    parity = tp % 2
    mate = y * 2 + (1 - c)
    pair = tp + 1 - 2 * parity

    barrier = pltpu.get_barrier_semaphore()

    def greet_ep(i):
        pl.semaphore_signal(
            barrier, inc=1, device_id={"ep": lax.rem(ep + 1 + i, n_ep)}, device_id_type=MESH
        )

    def greet_tp(i):
        pl.semaphore_signal(
            barrier, inc=1, device_id={"tp": lax.rem(tp + 1 + i, n_tp)}, device_id_type=MESH
        )

    each(n_ep - 1, greet_ep)
    each(n_tp - 1, greet_tp)

    own_rows = pl.ds(pl.multiple_of(c * rows, rows), rows)
    mate_rows = pl.ds(pl.multiple_of((1 - c) * rows, rows), rows)
    own_copy = pltpu.make_async_copy(tok_hbm, tok_all.at[y, own_rows], tok_sem.at[0])
    own_copy.start()
    loads = [
        pltpu.make_async_copy(src, dst, w_sem.at[i])
        for i, (src, dst) in enumerate([
            (hg, vg), (hu, vu), (cg, wg), (cu, wu),
            (cd, wd.at[pl.ds(0, cold * ff)]), (hd, wd.at[pl.ds(cold * ff, hot * ff)]),
        ])
    ]
    for load in loads:
        load.start()

    def coef_rows(e):
        return pl.ds(pl.multiple_of(8 * e, 8), 8)

    pl.semaphore_wait(barrier, n_ep - 1 + n_tp - 1)

    def remote(src, dst, sems, *at, **target):
        return pltpu.make_async_remote_copy(
            src_ref=src, dst_ref=dst, send_sem=sems.at[(0, *at)], recv_sem=sems.at[(1, *at)],
            device_id=target, device_id_type=MESH,
        )

    def block_rows(core, which, s):
        return pl.ds(pl.multiple_of(core * rows + which * half + s * run, run), run)

    def tok_y(j, s):
        there = lax.rem(y + 1 + j, ny)
        return remote(
            tok_hbm.at[pl.ds(pl.multiple_of(parity * half + s * run, run), run)],
            tok_all.at[y, block_rows(c, parity, s)],
            yt_sem, j, s, ep=there * 2 + c,
        )

    def source(j):
        return lax.rem(y + ny - 1 - j, ny)

    def landed_y(j, s):
        at = tok_all.at[source(j), block_rows(c, parity, s)]
        return remote(at, at, yt_sem, j, s, ep=lax.rem(y + 1 + j, ny) * 2 + c)

    def tok_z(j, s):
        at = tok_all.at[source(j), block_rows(c, parity, s)]
        return remote(at, at, zt_sem, j, s, tp=pair)

    def landed_z(j, s):
        at = tok_all.at[source(j), block_rows(c, 1 - parity, s)]
        return remote(at, at, zt_sem, j, s, tp=pair)

    def tok_c(j, q, s):
        which = parity if q == 0 else 1 - parity
        at = tok_all.at[source(j), block_rows(c, which, s)]
        return remote(at, at, ct_sem, j, q, s, ep=mate)

    def landed_c(j, q, s):
        which = parity if q == 0 else 1 - parity
        at = tok_all.at[source(j), block_rows(1 - c, which, s)]
        return remote(at, at, ct_sem, j, q, s, ep=mate)

    def coef_copy(i):
        e = lax.rem(ep + 1 + i, n_ep)
        return remote(
            coef_out.at[coef_rows(e)], coef_in.at[coef_rows(ep)], coef_sem, i, ep=e
        )

    def landed_coef(i):
        e = lax.rem(ep + n_ep - 1 - i, n_ep)
        return remote(
            coef_out.at[coef_rows(e)], coef_in.at[coef_rows(e)], coef_sem, i,
            ep=lax.rem(ep + 1 + i, n_ep),
        )

    block_copy = remote(tok_hbm, tok_all.at[y, own_rows], blk_sem, 0, ep=mate)
    block_landed = remote(tok_hbm, tok_all.at[y, mate_rows], blk_sem, 0, ep=mate)

    for s in range(FLIGHT):
        each(ny - 1, lambda j: tok_y(j, s).start())
    block_copy.start()

    ids = ids_ref[...].astype(jnp.float32).T.astype(jnp.int32)
    weights = weights_ref[...].T
    scaled = ROUTE_SCALE * weights / jnp.sum(weights, axis=1, keepdims=True)
    slot = ids
    hot_coef = []
    for h in range(hot):
        slot = slot - (hot_ref[h] < ids).astype(jnp.int32)
    for h in range(hot):
        match = ids == hot_ref[h]
        slot = jnp.where(match, -1, slot)
        hot_coef.append(jnp.sum(jnp.where(match, scaled, 0.0), axis=1, keepdims=True))
    lane = lax.broadcasted_iota(jnp.int32, (rows, 128), 1)
    lane_slot = jnp.where(lane % 8 < cold, (lane // 8) * cold + lane % 8, -2)
    table = jnp.zeros((rows, 128), jnp.float32)
    for k in range(ids.shape[1]):
        table = table + jnp.where(lane_slot == slot[:, k:k + 1], scaled[:, k:k + 1], 0.0)
    coef_out[...] = table.T

    each(n_ep - 1, lambda i: coef_copy(i).start())
    coef_in[coef_rows(ep), :] = coef_out[coef_rows(ep), :]

    def pass_on(s):
        def step(j):
            if s + FLIGHT < SPLITS:
                tok_y(j, s).wait_send()
                tok_y(j, s + FLIGHT).start()
            landed_y(j, s).wait_recv()
            tok_z(j, s).start()
            tok_c(j, 0, s).start()
        each(ny - 1, step)

    def pass_across(s):
        def step(j):
            landed_z(j, s).wait_recv()
            tok_c(j, 1, s).start()
        each(ny - 1, step)

    def act(x, gate, up, coef):
        g = jnp.dot(x, gate, preferred_element_type=jnp.float32)
        u = jnp.dot(x, up, preferred_element_type=jnp.float32)
        return (g / (1.0 + jnp.exp(-g)) * u * coef).astype(jnp.bfloat16)

    def cold_coef(yy, e):
        one = coef_in[coef_rows(yy * 2), :].T[:, e:e + 1]
        two = coef_in[coef_rows(yy * 2 + 1), :].T[:, e:e + 1]
        return jnp.concatenate([one, two], axis=0)

    def cold_hidden(yy, e):
        hid[yy, :, e * ff:(e + 1) * ff] = act(tok_all[yy], wg[e], wu[e], cold_coef(yy, e))

    own_copy.wait()
    loads[0].wait()
    loads[1].wait()
    for h in range(hot):
        hot_hid[:, h * ff:(h + 1) * ff] = act(
            tok_all[y, own_rows], vg[h], vu[h], hot_coef[h]
        )
        if h < 2:
            pass_on(h)
    loads[2].wait()
    loads[3].wait()
    block_landed.wait_recv()
    each(n_ep - 1, lambda i: landed_coef(i).wait_recv())
    begun = min(hot, 2)
    for e in range(cold):
        cold_hidden(y, e)
        if begun + e < SPLITS:
            pass_on(begun + e)
        if e < SPLITS:
            pass_across(e)
    for s in range(begun + cold, SPLITS):
        pass_on(s)
    for s in range(cold, SPLITS):
        pass_across(s)
    for s in range(SPLITS):
        each(ny - 1, lambda j: landed_c(j, 0, s).wait_recv())
    for s in range(SPLITS):
        each(ny - 1, lambda j: landed_c(j, 1, s).wait_recv())

    def far_hidden(j):
        for e in range(cold):
            cold_hidden(lax.rem(y + 1 + j, ny), e)

    each(ny - 1, far_hidden)
    loads[4].wait()
    loads[5].wait()

    def columns(k):
        t = lax.rem(tp + 1 + k, n_tp)
        return pl.ds(pl.multiple_of(t * piece, 128), piece)

    span = rows // PARTS

    def cut(r):
        return pl.ds(r * span, span)

    def core_copy(j, k, r):
        return remote(
            core_out.at[j, k, cut(r)], core_in.at[j, k, cut(r)], core_sem, j, k, r, ep=mate
        )

    def y_copy(j, k, r):
        return remote(
            y_out.at[j, k, cut(r)], y_in.at[j, k, cut(r)], y_sem, j, k, r,
            ep=lax.rem(y + 1 + j, ny) * 2 + c,
        )

    def z_copy(k, r):
        return remote(
            z_out.at[k, cut(r)], z_in.at[k, cut(r)], z_sem, k, r, tp=lax.rem(tp + 1 + k, n_tp)
        )

    def project(j, k):
        yy = lax.rem(y + 1 + j, ny)
        part[...] = jnp.dot(
            hid[yy], wd[:cold * ff, columns(k)], preferred_element_type=jnp.float32
        )
        core_out[j, k] = part[mate_rows, :].astype(jnp.bfloat16)
        for r in range(PARTS):
            core_copy(j, k, r).start()

    def far(k):
        def step(j):
            project(j, k)
            for r in range(PARTS):
                keep = part[pl.ds(pl.multiple_of(c * rows + r * span, span), span), :]
                core_copy(j, k, r).wait_recv()
                y_out[j, k, cut(r)] = (
                    keep + core_in[j, k, cut(r)].astype(jnp.float32)
                ).astype(jnp.bfloat16)
        each(ny - 1, step)

    def send_y(k, r):
        def step(j):
            if k > 0:
                y_copy(j, k - 1, r).wait_send()
            y_copy(j, k, r).start()
        each(ny - 1, step)

    def near(k):
        project(ny - 1, k)
        own_part[k] = part[own_rows, :] + jnp.dot(
            hot_hid[...], wd[cold * ff:, columns(k)], preferred_element_type=jnp.float32
        )

    def total(k, r):
        core_copy(ny - 1, k, r).wait_recv()
        own_part[k, cut(r)] += core_in[ny - 1, k, cut(r)].astype(jnp.float32)

        def step(j):
            y_copy(j, k, r).wait_recv()
            own_part[k, cut(r)] += y_in[j, k, cut(r)].astype(jnp.float32)
        each(ny - 1, step)

    def hand_on(k, r):
        total(k, r)
        z_out[k, cut(r)] = own_part[k, cut(r)].astype(jnp.bfloat16)
        z_copy(k, r).start()

    for k in range(n_tp):
        far(k)
        send_y(k, 0)
        if k == 0:
            for r in range(1, PARTS):
                send_y(k, r)
        near(k)
        if k > 0:
            hand_on(k - 1, 0)
            for r in range(1, PARTS):
                send_y(k, r)
                hand_on(k - 1, r)
    for r in range(PARTS):
        total(n_tp - 1, r)

    def collect(k):
        for r in range(PARTS):
            z_copy(k, r).wait_recv()
            own_part[n_tp - 1, cut(r)] += z_in[k, cut(r)].astype(jnp.float32)

    each(n_tp - 1, collect)
    out_ref[...] = own_part[n_tp - 1].astype(out_ref.dtype)

    block_copy.wait_send()
    each(n_ep - 1, lambda i: coef_copy(i).wait_send())
    for s in range(SPLITS):
        def sent(j):
            if s + FLIGHT >= SPLITS:
                tok_y(j, s).wait_send()
            tok_z(j, s).wait_send()
            tok_c(j, 0, s).wait_send()
            tok_c(j, 1, s).wait_send()
        each(ny - 1, sent)

    def sums_sent(k):
        for r in range(PARTS):
            each(ny, lambda j: core_copy(j, k, r).wait_send())

    each(n_tp, sums_sent)
    for r in range(PARTS):
        each(ny - 1, lambda j: y_copy(j, n_tp - 1, r).wait_send())
        each(n_tp - 1, lambda k: z_copy(k, r).wait_send())


def per_device(
    n_ep, n_tp,
    tokens, expert_ids, route_weights, hot_list,
    cold_gate, cold_up, cold_down, hot_gate, hot_up, hot_down,
):
    rows, width = tokens.shape
    cold, _, ff = cold_gate.shape
    hot = hot_gate.shape[0]
    ny = n_ep // 2
    piece = width // n_tp
    padded = -(-piece // 128) * 128

    def flat(down):
        down = down.reshape(-1, n_tp, piece)
        if padded != piece:
            down = jnp.pad(down, ((0, 0), (0, 0), (0, padded - piece)))
        return down.reshape(-1, n_tp * padded)

    bf16, f32 = jnp.bfloat16, jnp.float32
    dma = pltpu.SemaphoreType.DMA
    vmem = pl.BlockSpec(memory_space=pltpu.VMEM)
    hbm = pl.BlockSpec(memory_space=pl.ANY)
    out = pl.pallas_call(
        functools.partial(layer_kernel, n_ep, n_tp),
        out_shape=jax.ShapeDtypeStruct((rows, padded), bf16),
        in_specs=[hbm, vmem, vmem, pl.BlockSpec(memory_space=pltpu.SMEM)] + [hbm] * 6,
        out_specs=vmem,
        scratch_shapes=[
            pltpu.VMEM((ny, 2 * rows, width), bf16),
            pltpu.VMEM((cold, width, ff), bf16),
            pltpu.VMEM((cold, width, ff), bf16),
            pltpu.VMEM((hot, width, ff), bf16),
            pltpu.VMEM((hot, width, ff), bf16),
            pltpu.VMEM(((cold + hot) * ff, n_tp * padded), bf16),
            pltpu.VMEM((ny, 2 * rows, cold * ff), bf16),
            pltpu.VMEM((rows, hot * ff), bf16),
            pltpu.VMEM((128, rows), f32),
            pltpu.VMEM((128, rows), f32),
            pltpu.VMEM((2 * rows, padded), f32),
            pltpu.VMEM((n_tp, rows, padded), f32),
            pltpu.VMEM((ny, n_tp, rows, padded), bf16),
            pltpu.VMEM((ny, n_tp, rows, padded), bf16),
            pltpu.VMEM((ny - 1, n_tp, rows, padded), bf16),
            pltpu.VMEM((ny - 1, n_tp, rows, padded), bf16),
            pltpu.VMEM((n_tp - 1, rows, padded), bf16),
            pltpu.VMEM((n_tp - 1, rows, padded), bf16),
            dma((6,)),
            dma((1,)),
            dma((2, n_ep - 1)),
            dma((2, 1)),
            dma((2, ny - 1, SPLITS)),
            dma((2, ny - 1, SPLITS)),
            dma((2, ny - 1, 2, SPLITS)),
            dma((2, ny, n_tp, PARTS)),
            dma((2, ny - 1, n_tp, PARTS)),
            dma((2, n_tp - 1, PARTS)),
        ],
        compiler_params=pltpu.CompilerParams(
            collective_id=0, has_side_effects=True, vmem_limit_bytes=63 * 1024 * 1024
        ),
        cost_estimate=pl.CostEstimate(
            flops=2 * rows * (n_ep * cold + hot) * 3 * width * ff,
            bytes_accessed=2 * 3 * (cold + hot) * width * ff,
            transcendentals=rows * (n_ep * cold + hot) * ff,
        ),
    )(
        tokens, expert_ids.T, route_weights.T, hot_list,
        cold_gate, cold_up, flat(cold_down), hot_gate, hot_up, flat(hot_down),
    )
    return out[:, :piece]


def solution(mesh):
    placed = (
        P(("groups", "ep"), None),
        P(("groups", "ep"), None),
        P(("groups", "ep"), None),
        P("groups"),
        P("ep", None, "tp"),
        P("ep", None, "tp"),
        P("ep", "tp", None),
        P(None, None, "tp"),
        P(None, None, "tp"),
        P(None, "tp", None),
    )
    return jax.shard_map(
        functools.partial(per_device, mesh.shape["ep"], mesh.shape["tp"]),
        mesh=mesh, in_specs=placed, out_specs=P(("groups", "ep"), "tp"), check_vma=False,
    )
```
